256 devices in a mesh: pb: 16 (over y_hi, z), ka: 16 (over x, y_lo, core).
Axes of the slice: x: 4, y: 4 (y_hi: 2, y_lo: 2; y = y_hi * 2 + y_lo), z: 8, core: 2. Of those that a mesh axis runs over, the one named last changes fastest.
Arguments:
- tokens: bfloat16 [16, 2048, 768], P('ka', 'pb'), may hold values from -6 to 6
- pair: bfloat16 [2048, 2048, 128], P('pb', 'ka'), may hold values from -500 to 500
- token_chain_index: int32 [2048], replicated, may hold values from 0 to 7, never falling along the last dimension, each value on 1 to 1024 neighbouring positions
- key_mask: int32 [2048], replicated, may hold values 0 or 1
- norm_gain: float32 [768], replicated, may hold values from 0.25 to 1.75
- pair_gain: float32 [128], replicated, may hold values from 0.1 to 1.9
- pair_proj: float32 [128, 16], replicated, may hold values from -0.140625 to 0.140625
- chain_gain: float32 [16], replicated, may hold values from -2 to 260
- w_qkvg: bfloat16 [768, 3072], replicated, may hold values from -0.21875 to 0.21875
- w_out: bfloat16 [768, 768], replicated, may hold values from -1.75 to 1.75
Outputs:
- update: bfloat16 [16, 2048, 768], P('ka', 'pb')
The draws below stay inside these ranges and needn't reach their ends.
Inputs may be any that keep to these rules, and one draw needn't show every extreme that they name: `token_chain_index`: chain ids never fall along the tokens.
All inputs are finite; a program needn't handle non-finite values.
Results may differ from the reference program's by a relative error of at most 0.02.
Values may be sent and summed in bfloat16 or wider, within the bound.
No kernel may reach another device: no remote copies, remote signals or barrier semaphores. Data moves between devices by JAX's collectives and lax.ppermute only.
A program may use at most 128 MiB of HBM per device.

```python
import math
import jax
import jax.numpy as jnp
import numpy as np
from jax import lax

D = 768
HEADS = 16
CZ = 128
QBLK = 128
CHAINS = 8
TOKENS = 2048
SAMPLES = 16


def draw_pair(key, part):
    key = jax.random.fold_in(key, 11)
    key_base, key_chan, key_cell = jax.random.split(key, 3)
    chan_scale = jnp.exp(jax.random.uniform(key_chan, (CZ,), jnp.float32, 0.0, math.log(10.0)))
    cell_scale = jnp.exp(jax.random.uniform(key_cell, (TOKENS, TOKENS, 1), jnp.float32, 0.0, math.log(10.0)))
    base = jnp.clip(jax.random.normal(key_base, (TOKENS, TOKENS, CZ), jnp.float32), -5.0, 5.0)
    return (base * chan_scale * cell_scale).astype(jnp.bfloat16)


def draw_pair_proj(key, part):
    key = jax.random.fold_in(key, 12)
    values = jnp.clip(jax.random.normal(key, (CZ, HEADS), jnp.float32), -3.0, 3.0) * (6.0 / CZ)
    return values


def draw_chain_gain(key, part):
    key = jax.random.fold_in(key, 13)
    key_small = jax.random.fold_in(key, 0)
    small = jax.random.uniform(key_small, (HEADS,), jnp.float32, -2.0, 2.0)
    values = small
    return values


def place_ends(drawn, stream_key, low, top_value):
    extent = drawn.shape
    spot = [jax.random.randint(jax.random.fold_in(stream_key, axis), (), 0, extent[axis]) for axis in range(len(extent))]
    drawn = drawn.at[tuple(spot)].set(low)
    longest = extent.index(max(extent))
    spot[longest] = (spot[longest] + 1) % extent[longest]
    return drawn.at[tuple(spot)].set(top_value)


def block_levels(stream_key, dims, pieces, least, high):
    def one(position, shards_of):
        draws = jax.random.uniform(jax.random.fold_in(jax.random.fold_in(stream_key, 6), position), (shards_of,), jnp.float32, least / len(pieces), high / len(pieces))
        return jnp.repeat(jnp.exp(draws), dims[position] // shards_of).reshape((-1,) + (1,) * (len(dims) - position - 1))

    factor_of = one(*pieces[0])
    for cut in pieces[1:]:
        factor_of = factor_of * one(*cut)
    return factor_of


def profile(amount, total, most, lean):
    portions = [(1 << 20) // math.isqrt(standing ** lean) + 1 for standing in range(2, amount + 1)]
    rest, counts = total - most - (amount - 1), [1] * (amount - 1)
    while rest > 0:
        candidates = [i for i in range(amount - 1) if counts[i] < most]
        mass, left = sum([portions[i] for i in candidates]), rest
        for i in candidates:
            extra = min(most - counts[i], max(1, left * portions[i] // mass), rest)
            counts[i] = counts[i] + extra
            rest = rest - extra
    return np.array([most] + counts)


def ragged(key, amount, total, reach, slope):
    if amount == 2:
        one = jax.random.randint(key, (), max(1, total - reach), min(reach, total - 1) + 1)
        return jnp.stack([one, total - one])
    sizes = jnp.asarray(profile(amount, total, reach, slope), jnp.int32)
    pairs = (amount - 1) // 2
    source_of, sink = sizes[1:1 + 2 * pairs:2], sizes[2:2 + 2 * pairs:2]
    room = jnp.minimum(source_of - 1, reach - sink)
    shifted = jax.random.randint(jax.random.fold_in(key, 1), (pairs,), 0, 1 << 20) % (room + 1)
    sizes = sizes.at[1:1 + 2 * pairs:2].set(source_of - shifted).at[2:2 + 2 * pairs:2].set(sink + shifted)
    return sizes[jax.random.permutation(jax.random.fold_in(key, 2), amount)]


def scatter_about(own_key, dims, deviation, reach, pieces=(), kind=jnp.bfloat16):
    level = block_levels(own_key, dims, pieces, -0.22, 0.18) if pieces else 1.0
    result = jax.random.normal(own_key, dims, jnp.float32) * deviation * level
    return jnp.minimum(jnp.maximum(result, -reach), reach).astype(kind)


def setup_inputs(seed: int = 0) -> dict:
    seeds = jax.random.split(jax.random.key(seed), 11)
    return {
        "tokens": scatter_about(seeds[0], (SAMPLES, TOKENS, D), 1.0, 6.0, ((0, 16), (1, 16))),
        "pair": draw_pair(jax.random.fold_in(seeds[10], 71), 0),
        "token_chain_index": jnp.searchsorted(jnp.cumsum(ragged(seeds[2], CHAINS, TOKENS, TOKENS // 2, 2)), jnp.arange(TOKENS), side="right").astype(jnp.int32),
        "key_mask": place_ends((jax.random.randint(seeds[3], (TOKENS,), 0, 8) < 7).astype(jnp.int32), jax.random.fold_in(seeds[3], 1), 0, 1),
        "norm_gain": jnp.clip(1.0 + 0.15 * jax.random.normal(seeds[4], (D,), jnp.float32), 0.25, 1.75),
        "pair_gain": jnp.clip(1.0 + 0.18 * jax.random.normal(seeds[5], (CZ,), jnp.float32), 0.1, 1.9),
        "pair_proj": draw_pair_proj(jax.random.fold_in(seeds[10], 71), 0),
        "chain_gain": draw_chain_gain(jax.random.fold_in(seeds[10], 71), 0),
        "w_qkvg": scatter_about(seeds[8], (D, 4 * D), D ** -0.5, 0.21875),
        "w_out": scatter_about(seeds[9], (D, D), (D // 64) ** -0.5, 1.75),
    }


epsilon = 1e-05

def norm_rows(values, gain):
    values = values.astype(jnp.float32)
    center = lax.optimization_barrier(jnp.mean(values, axis=-1, keepdims=True))
    spread = lax.optimization_barrier(jnp.mean(jnp.square(values - center), axis=-1, keepdims=True))
    return (values - center) * lax.rsqrt(spread + epsilon) * gain

def pair_bias(pair_rows, pair_gain, pair_proj, chain_query, chain_keys, chain_gain):
    zhat = norm_rows(pair_rows, pair_gain)
    head_bias = jnp.einsum('qkc,ch->hqk', zhat, pair_proj, precision=lax.Precision.HIGHEST)
    same = (chain_query[:, None] == chain_keys[None, :]).astype(jnp.float32)
    return head_bias + chain_gain[:, None, None] * same[None]

def apply_attention(query_vectors, keys, values, bias, key_mask):
    heads = bias.shape[0]
    q_count = query_vectors.shape[0]
    k_count = keys.shape[0]
    width = query_vectors.shape[1]
    hdim = width // heads
    query_heads = query_vectors.reshape(q_count, heads, hdim).astype(jnp.float32)
    key_heads = keys.reshape(k_count, heads, hdim).astype(jnp.float32)
    value_heads = values.reshape(k_count, heads, hdim).astype(jnp.float32)
    scores = jnp.einsum('qhd,khd->hqk', query_heads, key_heads) * hdim ** (-0.5) + bias
    scores = jnp.where(key_mask[None, None, :] > 0, scores, jnp.float32(-1000000000.0))
    top = lax.optimization_barrier(jnp.max(scores, axis=-1, keepdims=True))
    expo = jnp.exp(scores - top)
    total = lax.optimization_barrier(jnp.sum(expo, axis=-1))
    expo_b = lax.optimization_barrier(expo.astype(jnp.bfloat16)).astype(jnp.float32)
    summed = jnp.einsum('hqk,khd->qhd', expo_b, value_heads)
    return (summed / jnp.transpose(total)[:, :, None]).reshape(q_count, width)

def reference(tokens, pair, token_chain_index, key_mask, norm_gain, pair_gain, pair_proj, chain_gain, w_qkvg, w_out):
    normalized_input = norm_rows(tokens, norm_gain).astype(jnp.bfloat16)
    projected = jnp.dot(normalized_input.reshape(-1, D), w_qkvg, preferred_element_type=jnp.float32)
    projected = projected.reshape(SAMPLES, TOKENS, 4 * D)
    query_vectors = projected[:, :, :D].astype(jnp.bfloat16)
    keys = projected[:, :, D:2 * D].astype(jnp.bfloat16)
    values = projected[:, :, 2 * D:3 * D].astype(jnp.bfloat16)
    gate_values = projected[:, :, 3 * D:].astype(jnp.bfloat16)
    blocks = TOKENS // QBLK

    def pair_bias_tile(items):
        pair_block, chain_block = items
        return pair_bias(pair_block, pair_gain, pair_proj, chain_block, token_chain_index, chain_gain)
    bias_parts = lax.map(pair_bias_tile, (pair.reshape(blocks, QBLK, TOKENS, CZ), token_chain_index.reshape(blocks, QBLK)))
    bias = jnp.moveaxis(bias_parts, 0, 1).reshape(HEADS, TOKENS, TOKENS)

    def one_sample(items):
        query_one, key_one, value_one, gate_one = items
        attended = apply_attention(query_one, key_one, value_one, bias, key_mask)
        hidden = (jax.nn.sigmoid(gate_one.astype(jnp.float32)) * attended).astype(jnp.bfloat16)
        return jnp.dot(hidden, w_out, preferred_element_type=jnp.float32).astype(jnp.bfloat16)
    return lax.map(one_sample, (query_vectors, keys, values, gate_values))
```

```python
import functools
import math

import jax
import jax.numpy as jnp
from jax import lax
from jax.experimental import pallas as pl
from jax.experimental.pallas import tpu as pltpu
from jax.sharding import PartitionSpec as P

EPS = 1e-05
LOG2E = 1.4426950408889634
NEG = -1000000000.0 * LOG2E
F32 = jnp.float32
BF16 = jnp.bfloat16
MIB = 1024 * 1024


def dot(a, b, dims):
    return lax.dot_general(a, b, (dims, ((), ())), preferred_element_type=F32)


def params(mib):
    return pltpu.CompilerParams(vmem_limit_bytes=mib * MIB)


def norm_kernel(x_ref, gain_ref, out_ref):
    x = x_ref[...].astype(F32)
    center = jnp.mean(x, axis=-1, keepdims=True)
    d = x - center
    spread = jnp.mean(d * d, axis=-1, keepdims=True)
    out_ref[...] = (d * lax.rsqrt(spread + EPS) * gain_ref[...]).astype(BF16)


def norm_rows(x, gain):
    return pl.pallas_call(
        norm_kernel,
        out_shape=jax.ShapeDtypeStruct(x.shape, BF16),
        compiler_params=params(16),
    )(x, gain.reshape(1, -1))


def bias_kernel(pair_ref, gain_ref, proj_ref, out_ref, w_ref, swap_ref):
    nq, nk, nc = pair_ref.shape
    heads = out_ref.shape[0]

    @pl.when(pl.program_id(0) == 0)
    def _():
        w = proj_ref[...] * gain_ref[...] * LOG2E
        w = w - jnp.mean(w, axis=-1, keepdims=True)
        hi = w.astype(BF16)
        rest = w - hi.astype(F32)
        mid = rest.astype(BF16)
        low = (rest - mid.astype(F32)).astype(BF16)
        w_ref[...] = jnp.concatenate([hi, mid, low], axis=0)

    x = pair_ref[...].reshape(nq * nk, nc)
    ones = jnp.full((nc, nc), 1.0 / nc, BF16)
    center = dot(x, ones, ((1,), (0,)))
    d = x.astype(F32) - center
    d = d * d
    hi = d.astype(BF16)
    low = (d - hi.astype(F32)).astype(BF16)
    parts = jnp.concatenate([hi, low], axis=1)
    spread = dot(jnp.full((8, 2 * nc), 1.0 / nc, BF16), parts, ((1,), (1,)))[:1]
    r = dot(w_ref[...], x, ((1,), (1,)))
    r = r[:heads] + r[heads : 2 * heads] + r[2 * heads :]
    r = r * lax.rsqrt(spread + EPS)
    for q in range(nq):
        swap_ref[pl.ds(q, heads, stride=nq), :] = r[:, q * nk : (q + 1) * nk]
    out_ref[...] = swap_ref[...].reshape(heads, nq, nk).astype(BF16)


def pair_bias(pair, gain, proj_t, first, rows):
    nk, nc = pair.shape[1:]
    heads = proj_t.shape[0]
    step = 16
    return pl.pallas_call(
        bias_kernel,
        grid=(rows // step,),
        in_specs=[
            pl.BlockSpec((step, nk, nc), lambda i: (first // step + i, 0, 0)),
            pl.BlockSpec((1, nc), lambda i: (0, 0)),
            pl.BlockSpec((heads, nc), lambda i: (0, 0)),
        ],
        out_specs=pl.BlockSpec((heads, step, nk), lambda i: (0, i, 0)),
        out_shape=jax.ShapeDtypeStruct((heads, rows, nk), BF16),
        scratch_shapes=[pltpu.VMEM((3 * heads, nc), BF16), pltpu.VMEM((heads * step, nk), F32)],
        compiler_params=params(32),
        cost_estimate=pl.CostEstimate(
            flops=rows * nk * nc * 400, bytes_accessed=rows * nk * nc * 2, transcendentals=0
        ),
    )(pair, gain.reshape(1, -1), proj_t)


def kv_kernel(pos_ref, w_ref, *refs):
    blocks, out_ref = refs[:-1], refs[-1]
    rows = 256
    n = blocks[0].shape[0]
    for i in range(0, len(blocks), 2):
        x = jnp.concatenate([blocks[i][...], blocks[i + 1][...]], axis=0)
        at = [pl.multiple_of(pos_ref[i + j] * n, n) for j in range(2)]

        def one(m, _):
            m0 = pl.multiple_of(m * rows, rows)
            y = dot(w_ref[pl.ds(m0, rows), :], x, ((1,), (1,))).astype(BF16)
            for j in range(2):
                out_ref[pl.ds(m0, rows), pl.ds(at[j], n)] = y[:, j * n : (j + 1) * n]
            return 0

        lax.fori_loop(0, w_ref.shape[0] // rows, one, 0, unroll=True)


def keys_values(pos, w_t, blocks):
    n = blocks[0].shape[0]
    out = (w_t.shape[0], n * len(blocks))
    vmem = pl.BlockSpec(memory_space=pltpu.VMEM)
    return pl.pallas_call(
        kv_kernel,
        in_specs=[pl.BlockSpec(memory_space=pltpu.SMEM)] + [vmem] * (1 + len(blocks)),
        out_specs=vmem,
        out_shape=jax.ShapeDtypeStruct(out, BF16),
        compiler_params=params(40),
        cost_estimate=pl.CostEstimate(
            flops=2 * w_t.shape[0] * w_t.shape[1] * out[1], bytes_accessed=12 * MIB, transcendentals=0
        ),
    )(pos, w_t, *blocks)


def attend_kernel(scale, per, q_ref, k_ref, v_ref, bias_ref, chain_ref, mask_ref, gate_ref, w_ref, out_ref, hid_ref):
    step = pl.program_id(0)
    hdim = k_ref.shape[0] // per
    blocks = bias_ref.shape[0]
    for h in range(per):
        k = jnp.concatenate([k_ref[h * hdim : (h + 1) * hdim, :], chain_ref[...]], axis=0)
        s = dot(q_ref[h], k, ((1,), (0,))) * scale
        s = s + jnp.concatenate([bias_ref[c, h].astype(F32) for c in range(blocks)], axis=1)
        s = jnp.minimum(s, mask_ref[...])
        top = jnp.max(s, axis=-1, keepdims=True)
        p = jnp.exp2(s - top)
        total = jnp.sum(p, axis=-1, keepdims=True)
        o = dot(p.astype(BF16), v_ref[h * hdim : (h + 1) * hdim, :], ((1,), (1,)))
        o = o / total
        row = pl.multiple_of(step * (per * hdim) + h * hdim, 16)
        gate = gate_ref[pl.ds(row, hdim), :].astype(F32)
        hid_ref[pl.ds(row, hdim), :] = (jax.nn.sigmoid(gate) * o.T).astype(BF16)

    @pl.when(step == pl.num_programs(0) - 1)
    def _():
        out_ref[...] = dot(hid_ref[...], w_ref[...], ((0,), (0,))).astype(BF16)


def attend(q_aug, kv, bias, chain_rows, mask_row, gates_t, w_out):
    heads, nq, depth = q_aug.shape
    width = w_out.shape[0]
    hdim = width // heads
    keys = kv.shape[1]
    per = 4
    steps = heads // per
    scale = hdim**-0.5 * LOG2E
    whole = lambda *s: pl.BlockSpec(s, lambda i: (0,) * len(s))
    return pl.pallas_call(
        functools.partial(attend_kernel, scale, per),
        grid=(steps,),
        in_specs=[
            pl.BlockSpec((per, nq, depth), lambda i: (i, 0, 0)),
            pl.BlockSpec((per * hdim, keys), lambda i: (i, 0)),
            pl.BlockSpec((per * hdim, keys), lambda i: (i + steps, 0)),
            pl.BlockSpec((bias.shape[0], per, nq, bias.shape[3]), lambda i: (0, i, 0, 0)),
            whole(*chain_rows.shape),
            whole(*mask_row.shape),
            whole(*gates_t.shape),
            whole(*w_out.shape),
        ],
        out_specs=whole(nq, width),
        out_shape=jax.ShapeDtypeStruct((nq, width), BF16),
        scratch_shapes=[pltpu.VMEM((width, nq), BF16)],
        compiler_params=params(48),
        cost_estimate=pl.CostEstimate(
            flops=heads * nq * keys * 1024, bytes_accessed=heads * nq * keys * 2, transcendentals=heads * nq * keys
        ),
    )(q_aug, kv, kv, bias, chain_rows, mask_row, gates_t, w_out)


def shift_z(x, by):
    def to(i):
        return (i // 8) * 8 + (i % 8 + by) % 8

    return lax.ppermute(x, "pb", [(i, to(i)) for i in range(16)])


def swap_y(x):
    return lax.ppermute(x, "pb", [(i, (i + 8) % 16) for i in range(16)])


def gather_rows(own):
    me = lax.axis_index("pb")
    y, z = me // 8, me % 8
    other = swap_y(own)
    blocks, places = [own, other], [me, (1 - y) * 8 + z]
    for start, row, last in ((own, y, 1), (other, 1 - y, -1)):
        for by in (1, -1):
            now = start
            for hop in range(1, 5 if by == last else 4):
                now = shift_z(now, by)
                blocks.append(now)
                places.append(row * 8 + (z - by * hop) % 8)
    return blocks, jnp.stack(places).astype(jnp.int32)


def body(tokens, pair, token_chain_index, key_mask, norm_gain, pair_gain, pair_proj, chain_gain, w_qkvg, w_out):
    nq, width = tokens.shape[1:]
    heads = chain_gain.shape[0]
    hdim = width // heads
    keys = token_chain_index.shape[0]

    normed = norm_rows(tokens[0], norm_gain)
    proj_t = pair_proj.T
    half = nq // 2
    parts = [pair_bias(pair, pair_gain, proj_t, i * half, half) for i in range(2)]
    full = [lax.all_gather(b, "ka", axis=0, tiled=False) for b in parts]
    blocks, places = gather_rows(normed)

    w_t = w_qkvg.T
    kv = keys_values(places, w_t[width : 3 * width], blocks)

    q = dot(normed, w_qkvg[:, :width], ((1,), (0,))).astype(BF16)
    q = q.reshape(nq, heads, hdim).transpose(1, 0, 2)
    chain_query = lax.dynamic_slice_in_dim(token_chain_index, lax.axis_index("pb") * nq, nq)
    kinds = jnp.arange(8, dtype=jnp.int32)
    gain = chain_gain * math.sqrt(hdim)
    hi = gain.astype(BF16)
    rest = gain - hi.astype(F32)
    mid = rest.astype(BF16)
    low = (rest - mid.astype(F32)).astype(BF16)
    gains = jnp.stack([hi, mid, low, jnp.zeros_like(hi)], axis=1)
    hot_q = (chain_query[:, None] == kinds[None, :]).astype(BF16)
    chain_q = (gains[:, None, :, None] * hot_q[None, :, None, :]).reshape(heads, nq, 32)
    q_aug = jnp.concatenate([q, chain_q], axis=2)
    hot_k = (token_chain_index[None, :] == kinds[:, None]).astype(BF16)
    chain_rows = jnp.concatenate([hot_k] * 4, axis=0)
    mask_row = jnp.where(key_mask > 0, F32(3.0e38), F32(NEG)).reshape(1, keys)
    gates_t = dot(w_t[3 * width :], normed, ((1,), (1,))).astype(BF16)

    out = [
        attend(
            q_aug[:, i * half : (i + 1) * half],
            kv,
            full[i],
            chain_rows,
            mask_row,
            gates_t[:, i * half : (i + 1) * half],
            w_out,
        )
        for i in range(2)
    ]
    return jnp.concatenate(out, axis=0)[None]


def solution(mesh):
    in_specs = (P("ka", "pb", None), P("pb", "ka", None), P(), P(), P(), P(), P(), P(), P(), P())
    out_specs = P("ka", "pb", None)
    return jax.shard_map(body, mesh=mesh, in_specs=in_specs, out_specs=out_specs, check_vma=False)
```

```python
import functools

import jax
import jax.numpy as jnp
from jax import lax
from jax.experimental import pallas as pl
from jax.experimental.pallas import tpu as pltpu
from jax.sharding import PartitionSpec as P

EPS = 1e-05
LOG2E = 1.4426950408889634
NEG = -1000000000.0 * LOG2E
F32 = jnp.float32
BF16 = jnp.bfloat16
MIB = 1024 * 1024


def dot(a, b, dims):
    return lax.dot_general(a, b, (dims, ((), ())), preferred_element_type=F32)


def params(mib):
    return pltpu.CompilerParams(vmem_limit_bytes=mib * MIB)


def norm_kernel(x_ref, gain_ref, out_ref):
    x = x_ref[...].astype(F32)
    center = jnp.mean(x, axis=-1, keepdims=True)
    d = x - center
    spread = jnp.mean(d * d, axis=-1, keepdims=True)
    out_ref[...] = (d * lax.rsqrt(spread + EPS) * gain_ref[...]).astype(BF16)


def norm_rows(x, gain):
    return pl.pallas_call(
        norm_kernel,
        out_shape=jax.ShapeDtypeStruct(x.shape, BF16),
        compiler_params=params(61),
    )(x, gain.reshape(1, -1))


def bias_kernel(step, pair_ref, gain_ref, proj_ref, out_ref, x_ref, sem, swap_ref):
    rows, nk, nc = pair_ref.shape
    heads = proj_ref.shape[0]
    parts = rows // step

    def fetch(i):
        return pltpu.make_async_copy(pair_ref.at[pl.ds(i * step, step)], x_ref.at[pl.ds(i * step, step)], sem.at[i])

    for i in range(parts):
        fetch(i).start()

    w = proj_ref[...] * gain_ref[...] * LOG2E
    w = w - jnp.mean(w, axis=-1, keepdims=True)
    hi = w.astype(BF16)
    rest = w - hi.astype(F32)
    mid = rest.astype(BF16)
    low = (rest - mid.astype(F32)).astype(BF16)
    none = jnp.zeros((heads, nc), BF16)
    mean = jnp.full((heads, nc), 1.0 / nc, BF16)
    w = jnp.concatenate(
        [jnp.concatenate([hi, mid, low, none], axis=0), jnp.concatenate([none, none, none, mean], axis=0)], axis=1
    )
    row = lax.broadcasted_iota(jnp.int32, (nc, nc), 0)
    col = lax.broadcasted_iota(jnp.int32, (nc, nc), 1)
    center = (jnp.where(row == col, 1.0, 0.0) - 1.0 / nc).astype(BF16)

    for i in range(parts):
        fetch(i).wait()
        x = x_ref[i * step : (i + 1) * step].reshape(step * nk, nc)
        d = dot(x, center, ((1,), (0,)))
        r = dot(w, jnp.concatenate([x, (d * d).astype(BF16)], axis=1), ((1,), (1,)))
        spread = r[3 * heads : 3 * heads + 1]
        r = (r[:heads] + r[heads : 2 * heads] + r[2 * heads : 3 * heads]) * lax.rsqrt(spread + EPS)
        for q in range(step):
            swap_ref[pl.ds(i * step + q, heads, stride=rows), :] = r[:, q * nk : (q + 1) * nk]

    for h in range(heads):
        out_ref[:, h * rows : (h + 1) * rows] = swap_ref[h * rows : (h + 1) * rows, :].astype(BF16).T


def pair_bias(pair, gain, proj_t):
    rows, nk, nc = pair.shape
    heads = proj_t.shape[0]
    step = 16
    vmem = pl.BlockSpec(memory_space=pltpu.VMEM)
    return pl.pallas_call(
        functools.partial(bias_kernel, step),
        in_specs=[pl.BlockSpec(memory_space=pl.ANY), vmem, vmem],
        out_specs=vmem,
        out_shape=jax.ShapeDtypeStruct((nk, heads * rows), BF16),
        scratch_shapes=[
            pltpu.VMEM((rows, nk, nc), BF16),
            pltpu.SemaphoreType.DMA((rows // step,)),
            pltpu.VMEM((heads * rows, nk), F32),
        ],
        compiler_params=params(61),
        cost_estimate=pl.CostEstimate(
            flops=rows * nk * nc * 400, bytes_accessed=rows * nk * nc * 2, transcendentals=0
        ),
    )(pair, gain.reshape(1, -1), proj_t)


def whole(*s):
    return pl.BlockSpec(s, lambda i: (0,) * len(s))


def prepare_kernel(
    x_ref, wq_ref, wk_ref, wv_ref, wg_ref, chain_row_ref, chain_ref, mask_ref, gain_ref,
    q_ref, gate_ref, wide_ref, turned_ref, hot_ref, limit_ref,
):
    pairs, depth, lanes = q_ref.shape
    n = lanes // 2
    width = x_ref.shape[1]
    hdim = width // (2 * pairs)
    x = x_ref[...]
    q = (dot(wq_ref[...].T, x, ((1,), (1,))) * (hdim**-0.5 * LOG2E)).astype(BF16)
    gate_ref[...] = jax.nn.sigmoid(dot(wg_ref[...].T, x, ((1,), (1,))).astype(BF16).astype(F32))
    kinds = lax.broadcasted_iota(jnp.int32, (8, n), 0)
    same = kinds == chain_row_ref[...]
    none = jnp.zeros((hdim, n), BF16)
    for i in range(pairs):
        for j in range(2):
            h = 2 * i + j
            own = q[h * hdim : (h + 1) * hdim]
            gain = jnp.where(same, gain_ref[h] * LOG2E, 0.0)
            hi = gain.astype(BF16)
            rest = gain - hi.astype(F32)
            mid = rest.astype(BF16)
            low = (rest - mid.astype(F32)).astype(BF16)
            last = jnp.concatenate([hi, mid, low, jnp.zeros((depth - 2 * hdim - 24, n), BF16)], axis=0)
            q_ref[i, :, j * n : (j + 1) * n] = jnp.concatenate([none, own, last] if j else [own, none, last], axis=0)
    wide_ref[...] = jnp.zeros_like(wide_ref)
    for i in range(pairs):
        wide_ref[:, i * depth : i * depth + 2 * hdim] = wk_ref[:, 2 * i * hdim : (2 * i + 2) * hdim]
    turned_ref[...] = wv_ref[...].T
    step = 256
    lane = lax.broadcasted_iota(jnp.int32, (step, depth), 1) - 2 * hdim
    kind = jnp.where((lane >= 0) & (lane < 24), lane % 8, -1)
    for c in range(0, chain_ref.shape[0], step):
        hot_ref[c : c + step, :] = (chain_ref[c : c + step, :] == kind).astype(F32).astype(BF16)
        keep = jnp.broadcast_to(mask_ref[c : c + step, :], (step, limit_ref.shape[1]))
        limit_ref[c : c + step, :] = jnp.where(keep > 0, F32(3.0e38), F32(NEG))


def prepare(x, w, chain_index, chain_query, key_mask, chain_gain):
    n, width = x.shape
    heads = chain_gain.shape[0]
    keys = chain_index.shape[0]
    pairs, depth = heads // 2, 128
    shapes = [
        ((pairs, depth, 2 * n), BF16),
        ((width, n), F32),
        ((width, pairs * depth), BF16),
        ((width, width), BF16),
        ((keys, depth), BF16),
        ((keys, n), F32),
    ]
    return pl.pallas_call(
        prepare_kernel,
        grid=(1,),
        in_specs=[whole(n, width)]
        + [pl.BlockSpec((width, width), lambda i, j=j: (0, j)) for j in range(4)]
        + [whole(1, n), whole(keys, 1), whole(keys, 1), pl.BlockSpec(memory_space=pltpu.SMEM)],
        out_specs=[whole(*d) for d, _ in shapes],
        out_shape=[jax.ShapeDtypeStruct(d, t) for d, t in shapes],
        compiler_params=params(61),
        cost_estimate=pl.CostEstimate(flops=8 * n * width * width, bytes_accessed=12 * MIB, transcendentals=0),
    )(x, w, w, w, w, chain_query.reshape(1, n), chain_index.reshape(keys, 1), key_mask.reshape(keys, 1), chain_gain)


def kv_kernel(n, pos_ref, wide_ref, turned_ref, hot_ref, *refs):
    blocks, (k_ref, v_ref) = refs[:-2], refs[-2:]
    depth = hot_ref.shape[1]
    pairs = wide_ref.shape[1] // depth
    x = jnp.concatenate([b[...] for b in blocks], axis=0)
    for i in range(0, x.shape[0] // n, 2):
        rows = slice(i * n, (i + 2) * n)
        hot = jnp.concatenate(
            [hot_ref[pl.ds(pl.multiple_of(pos_ref[i + j] * n, n), n), :] for j in range(2)], axis=0
        )
        y = dot(x[rows], wide_ref[...], ((1,), (0,))).astype(BF16)
        k_ref[rows, :] = y + jnp.concatenate([hot] * pairs, axis=1)
        v_ref[:, rows] = dot(turned_ref[...], x[rows], ((1,), (1,))).astype(BF16)


def keys_values(pos, wide, turned, hot, blocks):
    tokens = sum(b.shape[0] for b in blocks)
    lanes, width = wide.shape[1], turned.shape[0]
    vmem = pl.BlockSpec(memory_space=pltpu.VMEM)
    return pl.pallas_call(
        functools.partial(kv_kernel, tokens // pos.shape[0]),
        in_specs=[pl.BlockSpec(memory_space=pltpu.SMEM)] + [vmem] * (3 + len(blocks)),
        out_specs=[vmem, vmem],
        out_shape=[
            jax.ShapeDtypeStruct((tokens, lanes), BF16),
            jax.ShapeDtypeStruct((width, tokens), BF16),
        ],
        compiler_params=params(61),
        cost_estimate=pl.CostEstimate(flops=5 * width * width * tokens, bytes_accessed=8 * MIB, transcendentals=0),
    )(pos, wide, turned, hot, *blocks)


def attend_kernel(n, batches, pos_ref, q_hbm, bias_ref, limit_hbm, gate_hbm, w_hbm, *refs):
    k_hbm, v_hbm = refs[:batches], refs[batches : 2 * batches]
    out_ref, q_ref, limit_ref, gate_ref, w_ref, k_ref, v_ref, b_ref, sem, hid_ref, s_ref, p_ref = refs[2 * batches :]
    pairs, depth, lanes = q_ref.shape
    nq = lanes // 2
    tokens = limit_ref.shape[0]
    hdim = w_ref.shape[0] // (2 * pairs)
    groups = b_ref.shape[0]
    per = pairs // groups
    starts = [0]
    for k in k_hbm:
        starts.append(starts[-1] + k.shape[0])

    def fetch(src, dst, i):
        return pltpu.make_async_copy(src, dst, sem.at[i])

    def fetch_keys(g):
        cols = slice(g * per * depth, (g + 1) * per * depth)
        return [
            fetch(k.at[:, cols], k_ref.at[starts[b] : starts[b + 1], cols], 4 + b * groups + g)
            for b, k in enumerate(k_hbm)
        ]

    def fetch_values(g):
        rows = slice(2 * g * per * hdim, 2 * (g + 1) * per * hdim)
        return [
            fetch(v.at[rows, :], v_ref.at[rows, starts[b] : starts[b + 1]], 4 + (batches + b) * groups + g)
            for b, v in enumerate(v_hbm)
        ]

    def bias_sem(g):
        return 4 + 2 * batches * groups + g

    fetch(q_hbm, q_ref, 0).start()
    fetch(limit_hbm, limit_ref, 1).start()
    for g in range(groups):
        for copy in fetch_keys(g):
            copy.start()
        cols = slice(g * per * lanes, (g + 1) * per * lanes)
        for c in range(tokens // n):
            at = pl.multiple_of(pos_ref[c] * n, n)
            fetch(bias_ref.at[pl.ds(at, n), cols], b_ref.at[g, pl.ds(c * n, n)], bias_sem(g)).start()
        for copy in fetch_values(g):
            copy.start()
        if g == 0:
            fetch(gate_hbm, gate_ref, 2).start()
    fetch(w_hbm, w_ref, 3).start()
    fetch(q_hbm, q_ref, 0).wait()
    fetch(limit_hbm, limit_ref, 1).wait()

    def scores(i):
        g, c0 = i // per, i % per * lanes
        if i % per == 0:
            for copy in fetch_keys(g):
                copy.wait()
            fetch(bias_ref.at[:, g * per * lanes : (g + 1) * per * lanes], b_ref.at[g], bias_sem(g)).wait()
        top = None
        for c in range(tokens // n):
            s = dot(k_ref[c * n : (c + 1) * n, i * depth : (i + 1) * depth], q_ref[i], ((1,), (0,)))
            mask = limit_ref[pl.ds(pl.multiple_of(pos_ref[c] * n, n), n), :]
            s = s + b_ref[g, c * n : (c + 1) * n, c0 : c0 + lanes].astype(F32)
            s = jnp.minimum(s, jnp.concatenate([mask, mask], axis=1))
            s_ref[i % 2, c * n : (c + 1) * n, :] = s
            t = jnp.max(s.reshape(n // 8, 8, lanes), axis=0)
            top = t if top is None else jnp.maximum(top, t)
        return jnp.max(top, axis=0, keepdims=True)

    def soften(i, top):
        total = None
        for c in range(tokens // n):
            p = jnp.exp2(s_ref[i % 2, c * n : (c + 1) * n, :] - top)
            p_ref[i % 2, c * n : (c + 1) * n, :] = p.astype(BF16)
            t = jnp.sum(p.reshape(n // 8, 8, lanes), axis=0)
            total = t if total is None else total + t
        return jnp.sum(total, axis=0, keepdims=True)

    def weigh(i, total):
        rows = slice(2 * i * hdim, (2 * i + 2) * hdim)
        if i == 0:
            fetch(gate_hbm, gate_ref, 2).wait()
        if i % per == 0:
            for copy in fetch_values(i // per):
                copy.wait()
        o = dot(v_ref[rows, :], p_ref[i % 2], ((1,), (0,))) / total
        o = jnp.concatenate([o[:hdim, :nq], o[hdim:, nq:]], axis=0)
        hid_ref[rows, :] = (gate_ref[rows, :] * o).astype(BF16)

    top = scores(0)
    for i in range(pairs):
        total = soften(i, top)
        if i + 1 < pairs:
            top = scores(i + 1)
        weigh(i, total)

    fetch(w_hbm, w_ref, 3).wait()
    out_ref[...] = dot(hid_ref[...], w_ref[...], ((0,), (0,))).astype(BF16)


def attend(pos, q, ks, vs, bias, limit, gates_t, w_out):
    pairs, _, lanes = q.shape
    width = w_out.shape[0]
    tokens = bias.shape[0]
    nq = lanes // 2
    groups = 4
    return pl.pallas_call(
        functools.partial(attend_kernel, tokens // pos.shape[0], len(ks)),
        in_specs=[pl.BlockSpec(memory_space=pltpu.SMEM)] + [pl.BlockSpec(memory_space=pl.ANY)] * (5 + 2 * len(ks)),
        out_specs=pl.BlockSpec(memory_space=pltpu.VMEM),
        out_shape=jax.ShapeDtypeStruct((nq, width), BF16),
        scratch_shapes=[
            pltpu.VMEM(q.shape, BF16),
            pltpu.VMEM(limit.shape, F32),
            pltpu.VMEM(gates_t.shape, F32),
            pltpu.VMEM(w_out.shape, BF16),
            pltpu.VMEM((tokens, ks[0].shape[1]), BF16),
            pltpu.VMEM((width, tokens), BF16),
            pltpu.VMEM((groups, tokens, pairs // groups * lanes), BF16),
            pltpu.SemaphoreType.DMA((4 + (2 * len(ks) + 1) * groups,)),
            pltpu.VMEM((width, nq), BF16),
            pltpu.VMEM((2, tokens, lanes), F32),
            pltpu.VMEM((2, tokens, lanes), BF16),
        ],
        compiler_params=params(61),
        cost_estimate=pl.CostEstimate(
            flops=pairs * lanes * tokens * 1024, bytes_accessed=8 * MIB, transcendentals=pairs * lanes * tokens
        ),
    )(pos, q, bias, limit, gates_t, w_out, *ks, *vs)


def shift_z(x, by):
    def to(i):
        return (i // 8) * 8 + (i % 8 + by) % 8

    return lax.ppermute(x, "pb", [(i, to(i)) for i in range(16)])


def swap_y(x):
    return lax.ppermute(x, "pb", [(i, (i + 8) % 16) for i in range(16)])


def attended_rows(own, prepared, bias, w_out):
    me = lax.axis_index("pb")
    y, z = me // 8, me % 8
    n = own.shape[0]
    both = jnp.concatenate([own, swap_y(own)], axis=0)

    def places(by):
        return [y * 8 + (z + by) % 8, (1 - y) * 8 + (z + by) % 8]

    ks, vs, pos = [], [], []

    def project(arrays, at):
        at = jnp.stack(at).astype(jnp.int32)
        k, v = keys_values(at, wide, turned, hot, arrays)
        ks.append(k)
        vs.append(v)
        pos.append(at)

    right, left = shift_z(both, 1), shift_z(both, -1)
    right, left, prepared = lax.optimization_barrier((right, left, prepared))
    q, gates_t, wide, turned, hot, limit = prepared
    waiting, at = [both, right, left], places(0) + places(-1) + places(1)
    for hop in range(2, 4):
        next_right, next_left = shift_z(right, 1), shift_z(left, -1)
        project(waiting, at)
        right, left, ks[-1], vs[-1] = lax.optimization_barrier((next_right, next_left, ks[-1], vs[-1]))
        waiting, at = [right, left], places(-hop) + places(hop)
    last = [shift_z(right[:n], 1), shift_z(left[n:], -1)]
    project(waiting, at)
    project(last, places(4))
    return attend(jnp.concatenate(pos), q, ks, vs, bias, limit, gates_t, w_out)


def body(tokens, pair, token_chain_index, key_mask, norm_gain, pair_gain, pair_proj, chain_gain, w_qkvg, w_out):
    nq = tokens.shape[1]

    normed = norm_rows(tokens[0], norm_gain)
    tile, normed = lax.optimization_barrier((pair, normed))
    bias = pair_bias(tile, pair_gain, pair_proj.T)
    bias_all = lax.all_gather(bias, "ka", axis=0, tiled=True)
    chain_query = lax.dynamic_slice_in_dim(token_chain_index, lax.axis_index("pb") * nq, nq)
    prepared = prepare(normed, w_qkvg, token_chain_index, chain_query, key_mask, chain_gain)
    return attended_rows(normed, prepared, bias_all, w_out)[None]


def solution(mesh):
    in_specs = (P("ka", "pb", None), P("pb", "ka", None), P(), P(), P(), P(), P(), P(), P(), P())
    out_specs = P("ka", "pb", None)
    return jax.shard_map(body, mesh=mesh, in_specs=in_specs, out_specs=out_specs, check_vma=False)
```

```python
import functools

import jax
import jax.numpy as jnp
from jax import lax
from jax.experimental import pallas as pl
from jax.experimental.pallas import tpu as pltpu
from jax.sharding import PartitionSpec as P

EPS = 1e-05
LOG2E = 1.4426950408889634
NEG = -1000000000.0 * LOG2E
F32 = jnp.float32
BF16 = jnp.bfloat16
MIB = 1024 * 1024


def dot(a, b, dims):
    return lax.dot_general(a, b, (dims, ((), ())), preferred_element_type=F32)


def params(mib):
    return pltpu.CompilerParams(vmem_limit_bytes=mib * MIB)


def norm_kernel(*refs):
    gain_ref, out_ref = refs[-2:]
    at = 0
    for x_ref in refs[:-2]:
        x = x_ref[...].astype(F32)
        center = jnp.mean(x, axis=-1, keepdims=True)
        d = x - center
        spread = jnp.mean(d * d, axis=-1, keepdims=True)
        out_ref[at : at + x.shape[0], :] = (d * lax.rsqrt(spread + EPS) * gain_ref[...]).astype(BF16)
        at += x.shape[0]


def norm_rows(parts, gain):
    rows = sum(x.shape[0] for x in parts)
    return pl.pallas_call(
        norm_kernel,
        out_shape=jax.ShapeDtypeStruct((rows, gain.shape[0]), BF16),
        compiler_params=params(61),
    )(*parts, gain.reshape(1, -1))


def bias_kernel(step, pair_ref, gain_ref, proj_ref, out_ref, x_ref, sem, swap_ref):
    rows, nk, nc = pair_ref.shape
    heads = proj_ref.shape[0]
    parts = rows // step

    def fetch(i):
        return pltpu.make_async_copy(pair_ref.at[pl.ds(i * step, step)], x_ref.at[pl.ds(i * step, step)], sem.at[i])

    for i in range(parts):
        fetch(i).start()

    w = proj_ref[...] * gain_ref[...] * LOG2E
    w = w - jnp.mean(w, axis=-1, keepdims=True)
    hi = w.astype(BF16)
    rest = w - hi.astype(F32)
    mid = rest.astype(BF16)
    low = (rest - mid.astype(F32)).astype(BF16)
    none = jnp.zeros((heads, nc), BF16)
    mean = jnp.full((heads, nc), 1.0 / nc, BF16)
    w = jnp.concatenate(
        [jnp.concatenate([hi, mid, low, none], axis=0), jnp.concatenate([none, none, none, mean], axis=0)], axis=1
    )
    row = lax.broadcasted_iota(jnp.int32, (nc, nc), 0)
    col = lax.broadcasted_iota(jnp.int32, (nc, nc), 1)
    center = (jnp.where(row == col, 1.0, 0.0) - 1.0 / nc).astype(BF16)

    for i in range(parts):
        fetch(i).wait()
        x = x_ref[i * step : (i + 1) * step].reshape(step * nk, nc)
        d = dot(x, center, ((1,), (0,)))
        r = dot(w, jnp.concatenate([x, (d * d).astype(BF16)], axis=1), ((1,), (1,)))
        spread = r[3 * heads : 3 * heads + 1]
        r = (r[:heads] + r[heads : 2 * heads] + r[2 * heads : 3 * heads]) * lax.rsqrt(spread + EPS)
        for q in range(step):
            swap_ref[pl.ds(i * step + q, heads, stride=rows), :] = r[:, q * nk : (q + 1) * nk]

    for h in range(heads):
        out_ref[:, h * rows : (h + 1) * rows] = swap_ref[h * rows : (h + 1) * rows, :].astype(BF16).T


def pair_bias(pair, gain, proj_t):
    rows, nk, nc = pair.shape
    heads = proj_t.shape[0]
    step = 32
    vmem = pl.BlockSpec(memory_space=pltpu.VMEM)
    return pl.pallas_call(
        functools.partial(bias_kernel, step),
        in_specs=[pl.BlockSpec(memory_space=pl.ANY), vmem, vmem],
        out_specs=vmem,
        out_shape=jax.ShapeDtypeStruct((nk, heads * rows), BF16),
        scratch_shapes=[
            pltpu.VMEM((rows, nk, nc), BF16),
            pltpu.SemaphoreType.DMA((rows // step,)),
            pltpu.VMEM((heads * rows, nk), F32),
        ],
        compiler_params=params(61),
        cost_estimate=pl.CostEstimate(
            flops=rows * nk * nc * 400, bytes_accessed=28 * MIB, transcendentals=0
        ),
    )(pair, gain.reshape(1, -1), proj_t)


def whole(*s):
    return pl.BlockSpec(s, lambda i: (0,) * len(s))


def prepare_kernel(
    x_ref, wq_ref, wk_ref, wv_ref, wg_ref, chain_row_ref, chain_ref, mask_ref, gain_ref,
    q_ref, gate_ref, wide_ref, turned_ref, hot_ref, limit_ref,
):
    pairs, depth, lanes = q_ref.shape
    n = lanes // 2
    width = x_ref.shape[1]
    hdim = width // (2 * pairs)
    x = x_ref[...]
    q = (dot(wq_ref[...].T, x, ((1,), (1,))) * (hdim**-0.5 * LOG2E)).astype(BF16)
    gate_ref[...] = jax.nn.sigmoid(dot(wg_ref[...].T, x, ((1,), (1,))).astype(BF16).astype(F32))
    kinds = lax.broadcasted_iota(jnp.int32, (8, n), 0)
    same = kinds == chain_row_ref[...]
    none = jnp.zeros((hdim, n), BF16)
    for i in range(pairs):
        for j in range(2):
            h = 2 * i + j
            own = q[h * hdim : (h + 1) * hdim]
            gain = jnp.where(same, gain_ref[h] * LOG2E, 0.0)
            hi = gain.astype(BF16)
            rest = gain - hi.astype(F32)
            mid = rest.astype(BF16)
            low = (rest - mid.astype(F32)).astype(BF16)
            last = jnp.concatenate([hi, mid, low, jnp.zeros((depth - 2 * hdim - 24, n), BF16)], axis=0)
            q_ref[i, :, j * n : (j + 1) * n] = jnp.concatenate([none, own, last] if j else [own, none, last], axis=0)
    wide_ref[...] = jnp.zeros_like(wide_ref)
    for i in range(pairs):
        wide_ref[:, i * depth : i * depth + 2 * hdim] = wk_ref[:, 2 * i * hdim : (2 * i + 2) * hdim]
    turned_ref[...] = wv_ref[...].T
    step = 256
    lane = lax.broadcasted_iota(jnp.int32, (step, depth), 1) - 2 * hdim
    kind = jnp.where((lane >= 0) & (lane < 24), lane % 8, -1)
    for c in range(0, chain_ref.shape[0], step):
        hot_ref[c : c + step, :] = (chain_ref[c : c + step, :] == kind).astype(F32).astype(BF16)
        keep = jnp.broadcast_to(mask_ref[c : c + step, :], (step, limit_ref.shape[1]))
        limit_ref[c : c + step, :] = jnp.where(keep > 0, F32(3.0e38), F32(NEG))


def prepare(x, w, chain_index, chain_query, key_mask, chain_gain):
    n, width = chain_query.shape[0], x.shape[1]
    heads = chain_gain.shape[0]
    keys = chain_index.shape[0]
    pairs, depth = heads // 2, 128
    shapes = [
        ((pairs, depth, 2 * n), BF16),
        ((width, n), F32),
        ((width, pairs * depth), BF16),
        ((width, width), BF16),
        ((keys, depth), BF16),
        ((keys, n), F32),
    ]
    return pl.pallas_call(
        prepare_kernel,
        grid=(1,),
        in_specs=[whole(n, width)]
        + [pl.BlockSpec((width, width), lambda i, j=j: (0, j)) for j in range(4)]
        + [whole(1, n), whole(keys, 1), whole(keys, 1), pl.BlockSpec(memory_space=pltpu.SMEM)],
        out_specs=[whole(*d) for d, _ in shapes],
        out_shape=[jax.ShapeDtypeStruct(d, t) for d, t in shapes],
        compiler_params=params(61),
        cost_estimate=pl.CostEstimate(flops=8 * n * width * width, bytes_accessed=12 * MIB, transcendentals=0),
    )(x, w, w, w, w, chain_query.reshape(1, n), chain_index.reshape(keys, 1), key_mask.reshape(keys, 1), chain_gain)


def kv_kernel(n, pos_ref, wide_ref, turned_ref, hot_ref, *refs):
    blocks, (k_ref, v_ref) = refs[:-2], refs[-2:]
    depth = hot_ref.shape[1]
    pairs = wide_ref.shape[1] // depth
    x = jnp.concatenate([b[...] for b in blocks], axis=0)
    for i in range(0, x.shape[0] // n, 2):
        rows = slice(i * n, (i + 2) * n)
        hot = jnp.concatenate(
            [hot_ref[pl.ds(pl.multiple_of(pos_ref[i + j] * n, n), n), :] for j in range(2)], axis=0
        )
        y = dot(x[rows], wide_ref[...], ((1,), (0,))).astype(BF16)
        k_ref[rows, :] = y + jnp.concatenate([hot] * pairs, axis=1)
        v_ref[:, rows] = dot(turned_ref[...], x[rows], ((1,), (1,))).astype(BF16)


def keys_values(pos, wide, turned, hot, blocks):
    tokens = sum(b.shape[0] for b in blocks)
    lanes, width = wide.shape[1], turned.shape[0]
    vmem = pl.BlockSpec(memory_space=pltpu.VMEM)
    return pl.pallas_call(
        functools.partial(kv_kernel, tokens // pos.shape[0]),
        in_specs=[pl.BlockSpec(memory_space=pltpu.SMEM)] + [vmem] * (3 + len(blocks)),
        out_specs=[vmem, vmem],
        out_shape=[
            jax.ShapeDtypeStruct((tokens, lanes), BF16),
            jax.ShapeDtypeStruct((width, tokens), BF16),
        ],
        compiler_params=params(61),
        cost_estimate=pl.CostEstimate(flops=5 * width * width * tokens, bytes_accessed=8 * MIB, transcendentals=0),
    )(pos, wide, turned, hot, *blocks)


def attend_kernel(n, batches, pos_ref, q_hbm, bias_ref, limit_hbm, gate_hbm, w_hbm, *refs):
    k_hbm, v_hbm = refs[:batches], refs[batches : 2 * batches]
    out_ref, q_ref, limit_ref, gate_ref, w_ref, k_ref, v_ref, b_ref, sem, hid_ref, s_ref, p_ref = refs[2 * batches :]
    pairs, depth, lanes = q_ref.shape
    nq = lanes // 2
    tokens = limit_ref.shape[0]
    hdim = w_ref.shape[0] // (2 * pairs)
    groups = b_ref.shape[0]
    per = pairs // groups
    starts = [0]
    for k in k_hbm:
        starts.append(starts[-1] + k.shape[0])

    def fetch(src, dst, i):
        return pltpu.make_async_copy(src, dst, sem.at[i])

    def fetch_keys(g):
        cols = slice(g * per * depth, (g + 1) * per * depth)
        return [
            fetch(k.at[:, cols], k_ref.at[starts[b] : starts[b + 1], cols], 4 + b * groups + g)
            for b, k in enumerate(k_hbm)
        ]

    def fetch_values(g):
        rows = slice(2 * g * per * hdim, 2 * (g + 1) * per * hdim)
        return [
            fetch(v.at[rows, :], v_ref.at[rows, starts[b] : starts[b + 1]], 4 + (batches + b) * groups + g)
            for b, v in enumerate(v_hbm)
        ]

    def bias_sem(g):
        return 4 + 2 * batches * groups + g

    fetch(q_hbm, q_ref, 0).start()
    fetch(limit_hbm, limit_ref, 1).start()
    for g in range(groups):
        for copy in fetch_keys(g):
            copy.start()
        cols = slice(g * per * lanes, (g + 1) * per * lanes)
        for c in range(tokens // n):
            at = pl.multiple_of(pos_ref[c] * n, n)
            fetch(bias_ref.at[pl.ds(at, n), cols], b_ref.at[g, pl.ds(c * n, n)], bias_sem(g)).start()
        for copy in fetch_values(g):
            copy.start()
        if g == 0:
            fetch(gate_hbm, gate_ref, 2).start()
    fetch(w_hbm, w_ref, 3).start()
    fetch(q_hbm, q_ref, 0).wait()
    fetch(limit_hbm, limit_ref, 1).wait()

    def await_keys(i):
        g = i // per
        if i % per == 0:
            for copy in fetch_keys(g):
                copy.wait()
            fetch(bias_ref.at[:, g * per * lanes : (g + 1) * per * lanes], b_ref.at[g], bias_sem(g)).wait()

    def score(i, c, top):
        g, c0 = i // per, i % per * lanes
        s = dot(k_ref[c * n : (c + 1) * n, i * depth : (i + 1) * depth], q_ref[i], ((1,), (0,)))
        limit = limit_ref[pl.ds(pl.multiple_of(pos_ref[c] * n, n), n), :]
        s = s + b_ref[g, c * n : (c + 1) * n, c0 : c0 + lanes].astype(F32)
        s = jnp.minimum(s, jnp.concatenate([limit, limit], axis=1))
        s_ref[i % 2, c * n : (c + 1) * n, :] = s
        t = jnp.max(s.reshape(n // 8, 8, lanes), axis=0)
        return t if top is None else jnp.maximum(top, t)

    def soften(i, c, top, total):
        p = jnp.exp2(s_ref[i % 2, c * n : (c + 1) * n, :] - top)
        p_ref[i % 2, c * n : (c + 1) * n, :] = p.astype(BF16)
        t = jnp.sum(p.reshape(n // 8, 8, lanes), axis=0)
        return t if total is None else total + t

    def weigh(i, total):
        rows = slice(2 * i * hdim, (2 * i + 2) * hdim)
        if i == 0:
            fetch(gate_hbm, gate_ref, 2).wait()
        if i % per == 0:
            for copy in fetch_values(i // per):
                copy.wait()
        o = dot(v_ref[rows, :], p_ref[i % 2], ((1,), (0,))) / total
        o = jnp.concatenate([o[:hdim, :nq], o[hdim:, nq:]], axis=0)
        hid_ref[rows, :] = (gate_ref[rows, :] * o).astype(BF16)

    chunks = range(tokens // n)
    await_keys(0)
    top = None
    for c in chunks:
        top = score(0, c, top)
    for i in range(pairs):
        if i + 1 < pairs:
            await_keys(i + 1)
        top = jnp.max(top, axis=0, keepdims=True)
        total = after = None
        for c in chunks:
            if i + 1 < pairs:
                after = score(i + 1, c, after)
            total = soften(i, c, top, total)
        top = after
        weigh(i, jnp.sum(total, axis=0, keepdims=True))

    fetch(w_hbm, w_ref, 3).wait()
    out_ref[...] = dot(hid_ref[...], w_ref[...], ((0,), (0,))).astype(BF16)


def attend(pos, q, ks, vs, bias, limit, gates_t, w_out):
    pairs, _, lanes = q.shape
    width = w_out.shape[0]
    tokens = bias.shape[0]
    nq = lanes // 2
    groups = 4
    return pl.pallas_call(
        functools.partial(attend_kernel, tokens // pos.shape[0], len(ks)),
        in_specs=[pl.BlockSpec(memory_space=pltpu.SMEM)] + [pl.BlockSpec(memory_space=pl.ANY)] * (5 + 2 * len(ks)),
        out_specs=pl.BlockSpec(memory_space=pltpu.VMEM),
        out_shape=jax.ShapeDtypeStruct((nq, width), BF16),
        scratch_shapes=[
            pltpu.VMEM(q.shape, BF16),
            pltpu.VMEM(limit.shape, F32),
            pltpu.VMEM(gates_t.shape, F32),
            pltpu.VMEM(w_out.shape, BF16),
            pltpu.VMEM((tokens, ks[0].shape[1]), BF16),
            pltpu.VMEM((width, tokens), BF16),
            pltpu.VMEM((groups, tokens, pairs // groups * lanes), BF16),
            pltpu.SemaphoreType.DMA((4 + (2 * len(ks) + 1) * groups,)),
            pltpu.VMEM((width, nq), BF16),
            pltpu.VMEM((2, tokens, lanes), F32),
            pltpu.VMEM((2, tokens, lanes), BF16),
        ],
        compiler_params=params(61),
        cost_estimate=pl.CostEstimate(
            flops=pairs * lanes * tokens * 1024, bytes_accessed=8 * MIB, transcendentals=pairs * lanes * tokens
        ),
    )(pos, q, bias, limit, gates_t, w_out, *ks, *vs)


def shift_z(x, by):
    def to(i):
        return (i // 8) * 8 + (i % 8 + by) % 8

    return lax.ppermute(x, "pb", [(i, to(i)) for i in range(16)])


def swap_y(x):
    return lax.ppermute(x, "pb", [(i, (i + 8) % 16) for i in range(16)])


def attended_rows(both, prepared, bias, w_out):
    me = lax.axis_index("pb")
    y, z = me // 8, me % 8
    n = both.shape[0] // 2

    def places(by):
        return [y * 8 + (z + by) % 8, (1 - y) * 8 + (z + by) % 8]

    ks, vs, pos = [], [], []

    def project(arrays, at):
        at = jnp.stack(at).astype(jnp.int32)
        k, v = keys_values(at, wide, turned, hot, arrays)
        ks.append(k)
        vs.append(v)
        pos.append(at)

    right, left = shift_z(both, 1), shift_z(both, -1)
    right, left, prepared = lax.optimization_barrier((right, left, prepared))
    q, gates_t, wide, turned, hot, limit = prepared
    waiting, at = [both, right, left], places(0) + places(-1) + places(1)
    for hop in range(2, 4):
        next_right, next_left = shift_z(right, 1), shift_z(left, -1)
        project(waiting, at)
        right, left, ks[-1], vs[-1] = lax.optimization_barrier((next_right, next_left, ks[-1], vs[-1]))
        waiting, at = [right, left], places(-hop) + places(hop)
    last = [shift_z(right[:n], 1), shift_z(left[n:], -1)]
    project(waiting, at)
    project(last, places(4))
    return attend(jnp.concatenate(pos), q, ks, vs, bias, limit, gates_t, w_out)


def body(tokens, pair, token_chain_index, key_mask, norm_gain, pair_gain, pair_proj, chain_gain, w_qkvg, w_out):
    nq = tokens.shape[1]

    other = swap_y(tokens[0])
    bias = pair_bias(pair, pair_gain, pair_proj.T)
    other, bias = lax.optimization_barrier((other, bias))
    bias_all = lax.all_gather(bias, "ka", axis=0, tiled=True)
    normed = norm_rows([tokens[0], other], norm_gain)
    chain_query = lax.dynamic_slice_in_dim(token_chain_index, lax.axis_index("pb") * nq, nq)
    prepared = prepare(normed, w_qkvg, token_chain_index, chain_query, key_mask, chain_gain)
    return attended_rows(normed, prepared, bias_all, w_out)[None]


def solution(mesh):
    in_specs = (P("ka", "pb", None), P("pb", "ka", None), P(), P(), P(), P(), P(), P(), P(), P())
    out_specs = P("ka", "pb", None)
    return jax.shard_map(body, mesh=mesh, in_specs=in_specs, out_specs=out_specs, check_vma=False)
```

```python
import functools

import jax
import jax.numpy as jnp
from jax import lax
from jax.experimental import pallas as pl
from jax.experimental.pallas import tpu as pltpu
from jax.sharding import PartitionSpec as P

EPS = 1e-05
LOG2E = 1.4426950408889634
NEG = -1000000000.0 * LOG2E
F32 = jnp.float32
BF16 = jnp.bfloat16
MIB = 1024 * 1024


def dot(a, b, dims):
    return lax.dot_general(a, b, (dims, ((), ())), preferred_element_type=F32)


def params(mib):
    return pltpu.CompilerParams(vmem_limit_bytes=mib * MIB)


def norm_kernel(*refs):
    gain_ref, out_ref = refs[-2:]
    at = 0
    for x_ref in refs[:-2]:
        x = x_ref[...].astype(F32)
        center = jnp.mean(x, axis=-1, keepdims=True)
        d = x - center
        spread = jnp.mean(d * d, axis=-1, keepdims=True)
        out_ref[at : at + x.shape[0], :] = (d * lax.rsqrt(spread + EPS) * gain_ref[...]).astype(BF16)
        at += x.shape[0]


def norm_rows(parts, gain):
    rows = sum(x.shape[0] for x in parts)
    return pl.pallas_call(
        norm_kernel,
        out_shape=jax.ShapeDtypeStruct((rows, gain.shape[0]), BF16),
        compiler_params=params(61),
    )(*parts, gain.reshape(1, -1))


def bias_kernel(step, pair_ref, gain_ref, proj_ref, out_ref, x_ref, sem, swap_ref):
    rows, nk, nc = pair_ref.shape
    heads = proj_ref.shape[0]
    parts = rows // step

    def fetch(i):
        return pltpu.make_async_copy(pair_ref.at[pl.ds(i * step, step)], x_ref.at[pl.ds(i * step, step)], sem.at[i])

    for i in range(parts):
        fetch(i).start()

    w = proj_ref[...] * gain_ref[...] * LOG2E
    w = w - jnp.mean(w, axis=-1, keepdims=True)
    hi = w.astype(BF16)
    rest = w - hi.astype(F32)
    mid = rest.astype(BF16)
    low = (rest - mid.astype(F32)).astype(BF16)
    none = jnp.zeros((heads, nc), BF16)
    mean = jnp.full((heads, nc), 1.0 / nc, BF16)
    w = jnp.concatenate(
        [jnp.concatenate([hi, mid, low, none], axis=0), jnp.concatenate([none, none, none, mean], axis=0)], axis=1
    )
    row = lax.broadcasted_iota(jnp.int32, (nc, nc), 0)
    col = lax.broadcasted_iota(jnp.int32, (nc, nc), 1)
    center = (jnp.where(row == col, 1.0, 0.0) - 1.0 / nc).astype(BF16)

    for i in range(parts):
        fetch(i).wait()
        x = x_ref[i * step : (i + 1) * step].reshape(step * nk, nc)
        d = dot(x, center, ((1,), (0,)))
        r = dot(w, jnp.concatenate([x, (d * d).astype(BF16)], axis=1), ((1,), (1,)))
        spread = r[3 * heads : 3 * heads + 1]
        r = (r[:heads] + r[heads : 2 * heads] + r[2 * heads : 3 * heads]) * lax.rsqrt(spread + EPS)
        for q in range(step):
            swap_ref[pl.ds(i * step + q, heads, stride=rows), :] = r[:, q * nk : (q + 1) * nk]

    for h in range(heads):
        out_ref[:, h * rows : (h + 1) * rows] = swap_ref[h * rows : (h + 1) * rows, :].astype(BF16).T


def pair_bias(pair, gain, proj_t):
    rows, nk, nc = pair.shape
    heads = proj_t.shape[0]
    step = 32
    vmem = pl.BlockSpec(memory_space=pltpu.VMEM)
    return pl.pallas_call(
        functools.partial(bias_kernel, step),
        in_specs=[pl.BlockSpec(memory_space=pl.ANY), vmem, vmem],
        out_specs=vmem,
        out_shape=jax.ShapeDtypeStruct((nk, heads * rows), BF16),
        scratch_shapes=[
            pltpu.VMEM((rows, nk, nc), BF16),
            pltpu.SemaphoreType.DMA((rows // step,)),
            pltpu.VMEM((heads * rows, nk), F32),
        ],
        compiler_params=params(61),
        cost_estimate=pl.CostEstimate(
            flops=rows * nk * nc * 400, bytes_accessed=28 * MIB, transcendentals=0
        ),
    )(pair, gain.reshape(1, -1), proj_t)


def whole(*s):
    return pl.BlockSpec(s, lambda i: (0,) * len(s))


def prepare_kernel(
    x_ref, wq_ref, wk_ref, wv_ref, wg_ref, chain_row_ref, chain_ref, mask_ref, gain_ref,
    q_ref, gate_ref, wide_ref, turned_ref, hot_ref, limit_ref,
):
    pairs, depth, lanes = q_ref.shape
    n = lanes // 2
    width = x_ref.shape[1]
    hdim = width // (2 * pairs)
    x = x_ref[...]
    q = (dot(wq_ref[...].T, x, ((1,), (1,))) * (hdim**-0.5 * LOG2E)).astype(BF16)
    gate_ref[...] = jax.nn.sigmoid(dot(wg_ref[...].T, x, ((1,), (1,))).astype(BF16).astype(F32))
    kinds = lax.broadcasted_iota(jnp.int32, (8, n), 0)
    same = kinds == chain_row_ref[...]
    none = jnp.zeros((hdim, n), BF16)
    for i in range(pairs):
        for j in range(2):
            h = 2 * i + j
            own = q[h * hdim : (h + 1) * hdim]
            gain = jnp.where(same, gain_ref[h] * LOG2E, 0.0)
            hi = gain.astype(BF16)
            rest = gain - hi.astype(F32)
            mid = rest.astype(BF16)
            low = (rest - mid.astype(F32)).astype(BF16)
            last = jnp.concatenate([hi, mid, low, jnp.zeros((depth - 2 * hdim - 24, n), BF16)], axis=0)
            q_ref[i, :, j * n : (j + 1) * n] = jnp.concatenate([none, own, last] if j else [own, none, last], axis=0)
    wide_ref[...] = jnp.zeros_like(wide_ref)
    for i in range(pairs):
        wide_ref[:, i * depth : i * depth + 2 * hdim] = wk_ref[:, 2 * i * hdim : (2 * i + 2) * hdim]
    turned_ref[...] = wv_ref[...].T
    lane = lax.broadcasted_iota(jnp.int32, (depth, depth), 1) - 2 * hdim
    kind = jnp.where((lane >= 0) & (lane < 24), lane % 8, -1).astype(F32)
    for c in range(0, chain_ref.shape[1], depth):
        chain = jnp.broadcast_to(chain_ref[:, c : c + depth].astype(F32), (depth, depth)).T
        hot_ref[c : c + depth, :] = (chain == kind).astype(F32).astype(BF16)
        limit = jnp.where(mask_ref[:, c : c + depth] > 0, F32(3.0e38), F32(NEG))
        limit_ref[c : c + depth, :] = jnp.broadcast_to(limit, (depth, depth)).T


def prepare(x, w, chain_index, chain_query, key_mask, chain_gain):
    n, width = chain_query.shape[0], x.shape[1]
    heads = chain_gain.shape[0]
    keys = chain_index.shape[0]
    pairs, depth = heads // 2, 128
    shapes = [
        ((pairs, depth, 2 * n), BF16),
        ((width, n), F32),
        ((width, pairs * depth), BF16),
        ((width, width), BF16),
        ((keys, depth), BF16),
        ((keys, depth), F32),
    ]
    return pl.pallas_call(
        prepare_kernel,
        grid=(1,),
        in_specs=[whole(n, width)]
        + [pl.BlockSpec((width, width), lambda i, j=j: (0, j)) for j in range(4)]
        + [whole(1, n), whole(1, keys), whole(1, keys), pl.BlockSpec(memory_space=pltpu.SMEM)],
        out_specs=[whole(*d) for d, _ in shapes],
        out_shape=[jax.ShapeDtypeStruct(d, t) for d, t in shapes],
        compiler_params=params(61),
        cost_estimate=pl.CostEstimate(flops=8 * n * width * width, bytes_accessed=12 * MIB, transcendentals=0),
    )(x, w, w, w, w, chain_query.reshape(1, n), chain_index.reshape(1, keys), key_mask.reshape(1, keys), chain_gain)


def kv_kernel(n, pos_ref, wide_ref, turned_ref, hot_ref, *refs):
    blocks, (k_ref, v_ref) = refs[:-2], refs[-2:]
    depth = hot_ref.shape[1]
    pairs = wide_ref.shape[1] // depth
    x = jnp.concatenate([b[...] for b in blocks], axis=0)
    for i in range(0, x.shape[0] // n, 2):
        rows = slice(i * n, (i + 2) * n)
        hot = jnp.concatenate(
            [hot_ref[pl.ds(pl.multiple_of(pos_ref[i + j] * n, n), n), :] for j in range(2)], axis=0
        )
        y = dot(x[rows], wide_ref[...], ((1,), (0,))).astype(BF16)
        k_ref[rows, :] = y + jnp.concatenate([hot] * pairs, axis=1)
        v_ref[:, rows] = dot(turned_ref[...], x[rows], ((1,), (1,))).astype(BF16)


def keys_values(pos, wide, turned, hot, blocks):
    tokens = sum(b.shape[0] for b in blocks)
    lanes, width = wide.shape[1], turned.shape[0]
    vmem = pl.BlockSpec(memory_space=pltpu.VMEM)
    return pl.pallas_call(
        functools.partial(kv_kernel, tokens // pos.shape[0]),
        in_specs=[pl.BlockSpec(memory_space=pltpu.SMEM)] + [vmem] * (3 + len(blocks)),
        out_specs=[vmem, vmem],
        out_shape=[
            jax.ShapeDtypeStruct((tokens, lanes), BF16),
            jax.ShapeDtypeStruct((width, tokens), BF16),
        ],
        compiler_params=params(61),
        cost_estimate=pl.CostEstimate(flops=5 * width * width * tokens, bytes_accessed=8 * MIB, transcendentals=0),
    )(pos, wide, turned, hot, *blocks)


def attend_kernel(n, batches, pos_ref, q_hbm, bias_ref, limit_hbm, gate_hbm, w_hbm, *refs):
    k_hbm, v_hbm = refs[:batches], refs[batches : 2 * batches]
    out_ref, q_ref, limit_ref, gate_ref, w_ref, k_ref, v_ref, b_ref, sem, hid_ref, s_ref, p_ref = refs[2 * batches :]
    pairs, depth, lanes = q_ref.shape
    nq = lanes // 2
    tokens = limit_ref.shape[0]
    hdim = w_ref.shape[0] // (2 * pairs)
    runs = [(0, 1), (1, 2), (2, 4), (4, pairs)]
    groups = len(runs)
    first_of = {lo: g for g, (lo, _) in enumerate(runs)}
    starts = [0]
    for k in k_hbm:
        starts.append(starts[-1] + k.shape[0])

    def fetch(src, dst, i):
        return pltpu.make_async_copy(src, dst, sem.at[i])

    def fetch_keys(g):
        cols = slice(runs[g][0] * depth, runs[g][1] * depth)
        return [
            fetch(k.at[:, cols], k_ref.at[starts[b] : starts[b + 1], cols], 4 + b * groups + g)
            for b, k in enumerate(k_hbm)
        ]

    def fetch_values(g):
        rows = slice(2 * runs[g][0] * hdim, 2 * runs[g][1] * hdim)
        return [
            fetch(v.at[rows, :], v_ref.at[rows, starts[b] : starts[b + 1]], 4 + (batches + b) * groups + g)
            for b, v in enumerate(v_hbm)
        ]

    def bias_sem(g):
        return 4 + 2 * batches * groups + g

    def start_group(g):
        for copy in fetch_keys(g):
            copy.start()
        cols = slice(runs[g][0] * lanes, runs[g][1] * lanes)
        for c in range(tokens // n):
            at = pl.multiple_of(pos_ref[c] * n, n)
            fetch(bias_ref.at[pl.ds(at, n), cols], b_ref.at[pl.ds(c * n, n), cols], bias_sem(g)).start()
        for copy in fetch_values(g):
            copy.start()

    fetch(q_hbm, q_ref, 0).start()
    fetch(limit_hbm, limit_ref, 1).start()
    start_group(0)
    fetch(gate_hbm, gate_ref, 2).start()
    for g in range(1, groups):
        start_group(g)
    fetch(w_hbm, w_ref, 3).start()
    fetch(q_hbm, q_ref, 0).wait()
    fetch(limit_hbm, limit_ref, 1).wait()

    wide = [None]

    def await_keys(i):
        g = first_of.get(i)
        if g is not None:
            for copy in fetch_keys(g):
                copy.wait()
            cols = slice(runs[g][0] * lanes, runs[g][1] * lanes)
            fetch(bias_ref.at[:, cols], b_ref.at[:, cols], bias_sem(g)).wait()

    def score(i, c, top):
        if c * n % 256 == 0:
            wide[0] = dot(k_ref[c * n : c * n + 256, i * depth : (i + 1) * depth], q_ref[i], ((1,), (0,)))
        s = wide[0][c * n % 256 : c * n % 256 + n]
        limit = limit_ref[pl.ds(pl.multiple_of(pos_ref[c] * n, n), n), :]
        s = s + b_ref[c * n : (c + 1) * n, i * lanes : (i + 1) * lanes].astype(F32)
        s = jnp.minimum(s, jnp.concatenate([limit, limit], axis=1))
        s_ref[i % 2, c * n : (c + 1) * n, :] = s
        t = jnp.max(s.reshape(n // 8, 8, lanes), axis=0)
        return t if top is None else jnp.maximum(top, t)

    def soften(i, c, top, total):
        p = jnp.exp2(s_ref[i % 2, c * n : (c + 1) * n, :] - top)
        p_ref[i % 2, c * n : (c + 1) * n, :] = p.astype(BF16)
        t = jnp.sum(p.reshape(n // 8, 8, lanes), axis=0)
        return t if total is None else total + t

    def weigh(i, total):
        rows = slice(2 * i * hdim, (2 * i + 2) * hdim)
        if i == 0:
            fetch(gate_hbm, gate_ref, 2).wait()
        if i in first_of:
            for copy in fetch_values(first_of[i]):
                copy.wait()
        o = dot(v_ref[rows, :], p_ref[i % 2], ((1,), (0,))) / total
        o = jnp.concatenate([o[:hdim, :nq], o[hdim:, nq:]], axis=0)
        hid_ref[rows, :] = (gate_ref[rows, :] * o).astype(BF16)

    chunks = range(tokens // n)
    await_keys(0)
    top = None
    for c in chunks:
        top = score(0, c, top)
    for i in range(pairs):
        if i + 1 < pairs:
            await_keys(i + 1)
        top = jnp.max(top, axis=0, keepdims=True)
        total = after = None
        for c in chunks:
            if i + 1 < pairs:
                after = score(i + 1, c, after)
            total = soften(i, c, top, total)
        top = after
        weigh(i, jnp.sum(total, axis=0, keepdims=True))

    fetch(w_hbm, w_ref, 3).wait()
    out_ref[...] = dot(hid_ref[...], w_ref[...], ((0,), (0,))).astype(BF16)


def attend(pos, q, ks, vs, bias, limit, gates_t, w_out):
    pairs, _, lanes = q.shape
    width = w_out.shape[0]
    tokens = bias.shape[0]
    nq = lanes // 2
    groups = 4
    return pl.pallas_call(
        functools.partial(attend_kernel, tokens // pos.shape[0], len(ks)),
        in_specs=[pl.BlockSpec(memory_space=pltpu.SMEM)] + [pl.BlockSpec(memory_space=pl.ANY)] * (5 + 2 * len(ks)),
        out_specs=pl.BlockSpec(memory_space=pltpu.VMEM),
        out_shape=jax.ShapeDtypeStruct((nq, width), BF16),
        scratch_shapes=[
            pltpu.VMEM(q.shape, BF16),
            pltpu.VMEM(limit.shape, F32),
            pltpu.VMEM(gates_t.shape, F32),
            pltpu.VMEM(w_out.shape, BF16),
            pltpu.VMEM((tokens, ks[0].shape[1]), BF16),
            pltpu.VMEM((width, tokens), BF16),
            pltpu.VMEM((tokens, pairs * lanes), BF16),
            pltpu.SemaphoreType.DMA((4 + (2 * len(ks) + 1) * groups,)),
            pltpu.VMEM((width, nq), BF16),
            pltpu.VMEM((2, tokens, lanes), F32),
            pltpu.VMEM((2, tokens, lanes), BF16),
        ],
        compiler_params=params(61),
        cost_estimate=pl.CostEstimate(
            flops=pairs * lanes * tokens * 1024, bytes_accessed=8 * MIB, transcendentals=pairs * lanes * tokens
        ),
    )(pos, q, bias, limit, gates_t, w_out, *ks, *vs)


def shift_z(x, by):
    def to(i):
        return (i // 8) * 8 + (i % 8 + by) % 8

    return lax.ppermute(x, "pb", [(i, to(i)) for i in range(16)])


def swap_y(x):
    return lax.ppermute(x, "pb", [(i, (i + 8) % 16) for i in range(16)])


def attended_rows(both, prepared, bias, w_out):
    me = lax.axis_index("pb")
    y, z = me // 8, me % 8
    n = both.shape[0] // 2

    def places(by):
        return [y * 8 + (z + by) % 8, (1 - y) * 8 + (z + by) % 8]

    ks, vs, pos = [], [], []

    def project(arrays, at):
        at = jnp.stack(at).astype(jnp.int32)
        k, v = keys_values(at, wide, turned, hot, arrays)
        ks.append(k)
        vs.append(v)
        pos.append(at)

    right, left = shift_z(both, 1), shift_z(both, -1)
    right, left, prepared = lax.optimization_barrier((right, left, prepared))
    q, gates_t, wide, turned, hot, limit = prepared
    waiting, at = [both, right, left], places(0) + places(-1) + places(1)
    for hop in range(2, 4):
        next_right, next_left = shift_z(right, 1), shift_z(left, -1)
        project(waiting, at)
        right, left, ks[-1], vs[-1] = lax.optimization_barrier((next_right, next_left, ks[-1], vs[-1]))
        waiting, at = [right, left], places(-hop) + places(hop)
    last = [shift_z(right[:n], 1), shift_z(left[n:], -1)]
    project(waiting, at)
    project(last, places(4))
    return attend(jnp.concatenate(pos), q, ks, vs, bias, limit, gates_t, w_out)


def body(tokens, pair, token_chain_index, key_mask, norm_gain, pair_gain, pair_proj, chain_gain, w_qkvg, w_out):
    nq = tokens.shape[1]

    other = swap_y(tokens[0])
    bias = pair_bias(pair, pair_gain, pair_proj.T)
    other, bias = lax.optimization_barrier((other, bias))
    bias_all = lax.all_gather(bias, "ka", axis=0, tiled=True)
    normed = norm_rows([tokens[0], other], norm_gain)
    chain_query = lax.dynamic_slice_in_dim(token_chain_index, lax.axis_index("pb") * nq, nq)
    prepared = prepare(normed, w_qkvg, token_chain_index, chain_query, key_mask, chain_gain)
    return attended_rows(normed, prepared, bias_all, w_out)[None]


def solution(mesh):
    in_specs = (P("ka", "pb", None), P("pb", "ka", None), P(), P(), P(), P(), P(), P(), P(), P())
    out_specs = P("ka", "pb", None)
    return jax.shard_map(body, mesh=mesh, in_specs=in_specs, out_specs=out_specs, check_vma=False)
```
